32 devices in a mesh: groups: 2 (over y), seg: 4 (over z), slab: 2 (over x), comp: 2 (over core).
Axes of the slice: x: 2, y: 2, z: 4, core: 2. Of those that a mesh axis runs over, the one named last changes fastest.
Arguments:
- base: float32 [8, 3, 64, 4096], P(('groups', 'seg'), None, 'slab'), parts along dimension 0, may hold values from -6 to 6
- state: float32 [8, 2, 3, 64, 4096], P(('groups', 'seg'), 'comp', None, 'slab'), parts along dimension 0, may hold values from -6 to 6
- wavenumber: int32 [2], P('groups'), parts along dimension 0, may hold values from 1 to 4
- cutoff: int32 [6], P('groups'), parts along dimension 0, may hold values from 18 to 21, as said below
Outputs:
- base_gap: float32 [8, 3, 64, 4096], P(('groups', 'seg'), None, ('slab', 'comp')), parts along dimension 0
- state_gap: float32 [8, 2, 3, 64, 4096], P(('groups', 'seg'), 'comp', None, 'slab'), parts along dimension 0
The draws below stay inside these ranges and needn't reach their ends.
There are 2 independent parts, one for each index of `groups`. The reference program is written for one: setup_inputs(seed, part) draws one part's arguments, and reference() takes and returns one part's arrays. A program takes and returns all parts, laid end to end along the dimension named above; each array names one. Nothing has to cross between parts.
Inputs may be any that keep to these rules, and one draw needn't show every extreme that they name: `cutoff`: each entry is at most one third of 64, rounded down, and at least that minus three; one entry always equals it.
All inputs are finite; a program needn't handle non-finite values.
Results may differ from the reference program's by a relative error of at most 0.0001.
Values sent between devices are 32-bit elements; how exact they have to be, the bound alone decides.
A program may use at most 128 MiB of HBM per device.

```python
import jax
import jax.numpy as jnp
from jax import lax

N = 64
SEG = 4


def draw_cutoff(key, part):
    first_key, second_key = jax.random.split(jax.random.fold_in(key, 17))
    offsets = jax.random.randint(first_key, (3,), 0, 4)
    chosen = jax.random.randint(second_key, (), 0, 3)
    offsets = jnp.where(jnp.arange(3) == chosen, 0, offsets)
    return (N // 3 - offsets).astype(jnp.int32)


def levels(stream_key, shape, pieces, least, top_value):
    factor_of, own = 1.0, jax.random.fold_in(stream_key, 6)
    for dim, parts in pieces:
        steps = jnp.exp(jax.random.uniform(jax.random.fold_in(own, dim), (parts,), jnp.float32, least / len(pieces), top_value / len(pieces)))
        factor_of = factor_of * jnp.repeat(steps, shape[dim] // parts).reshape([-1 if axis == dim else 1 for axis in range(len(shape))])
    return factor_of


def noise(own_key, dims, width, most, shards=(), kind=jnp.bfloat16):
    result = width * jax.random.normal(own_key, dims, jnp.float32)
    if shards:
        result = result * levels(own_key, dims, shards, -0.22, 0.18)
    return jnp.clip(result, -most, most).astype(kind)


def setup_inputs(seed: int = 0, part: int = 0) -> dict:
    keys = jax.random.split(jax.random.key(seed), 5)
    own_keys = jax.random.split(jax.random.fold_in(keys[4], part), 5)
    base = noise(own_keys[0], (SEG, 3, N, N * N), 1.0, 6.0, ((0, 4), (2, 2)), jnp.float32)
    state = noise(own_keys[1], (SEG, 2, 3, N, N * N), 1.0, 6.0, ((0, 4), (1, 2), (3, 2)), jnp.float32)
    wavenumber = jax.random.randint(own_keys[2], (1,), 1, 5).astype(jnp.int32)
    cutoff = draw_cutoff(jax.random.fold_in(jax.random.fold_in(keys[4], part), 71), part)
    return dict(base=base, state=state, wavenumber=wavenumber, cutoff=cutoff)


viscosity = 0.025
time_step = 0.02
forcing_amp = 10.0


def wavenumbers(grid_points):
    position = jnp.arange(grid_points, dtype=jnp.int32)
    return jnp.where(position < grid_points // 2, position, position - grid_points)


def transform(field):
    return jnp.fft.fftn(field, axes=(-3, -2, -1))


def restore(modes):
    return jnp.real(jnp.fft.ifftn(modes, axes=(-3, -2, -1)))


def reference(base, state, wavenumber, cutoff):
    base = base.reshape(SEG, 3, N, N, N)
    state = state.reshape(SEG, 2, 3, N, N, N)
    spectrum = wavenumbers(N)
    wave_x = jnp.broadcast_to(spectrum[:, None, None], (N, N, N))
    wave_y = jnp.broadcast_to(spectrum[None, :, None], (N, N, N))
    wave_z = jnp.broadcast_to(spectrum[None, None, :], (N, N, N))
    inside = (jnp.abs(wave_x) <= cutoff[0]) & (jnp.abs(wave_y) <= cutoff[1]) & (jnp.abs(wave_z) <= cutoff[2])
    keep_mask = inside.astype(jnp.float32)
    float_x = wave_x.astype(jnp.float32)
    float_y = wave_y.astype(jnp.float32)
    float_z = wave_z.astype(jnp.float32)
    waves_stack = jnp.stack([float_x, float_y, float_z])
    ksquare = float_x * float_x + float_y * float_y + float_z * float_z
    safe_square = jnp.where(ksquare > 0, ksquare, jnp.ones_like(ksquare))
    damping = 1.0 / (1.0 + viscosity * time_step * ksquare)

    def project(field):
        divergence = (float_x * field[0] + float_y * field[1] + float_z * field[2]) / safe_square
        return jnp.stack([field[0] - float_x * divergence, field[1] - float_y * divergence, field[2] - float_z * divergence])

    grid_index = jnp.arange(N, dtype=jnp.int32)
    phase = jnp.mod(wavenumber[0] * grid_index, N).astype(jnp.float32) * (2.0 * jnp.pi / N)
    forcing = jnp.broadcast_to(forcing_amp * jnp.sin(phase)[None, :, None], (N, N, N))

    def advance(segment):
        flow, paired = segment
        flow_hat = transform(flow) * keep_mask
        gradient = restore(1j * waves_stack[None, :] * flow_hat[:, None])
        base_drive = jnp.sum(gradient * flow[None, :], axis=1)
        base_drive = jnp.concatenate([base_drive[:1] - forcing[None], base_drive[1:]], axis=0)
        flow_new = restore(damping * project(flow_hat - time_step * keep_mask * transform(base_drive)))
        results = []
        for branch, orient in ((0, 1.0), (1, -1.0)):
            field = paired[branch]
            field_hat = transform(field) * keep_mask
            flux_hat = transform(field[:, None] * flow[None, :])
            divergence = jnp.sum(1j * waves_stack[None, :] * flux_hat, axis=1)
            if branch == 0:
                matrix = gradient
            else:
                matrix = jnp.swapaxes(gradient, 0, 1)
            coupling = jnp.sum(matrix * field[None, :], axis=1)
            state_drive = keep_mask * (orient * divergence + transform(coupling))
            results.append(restore(damping * project(field_hat - time_step * state_drive)))
        return flow_new, jnp.stack(results)

    flow_next, state_next = lax.map(advance, (base, state))
    base_gap = flow_next - jnp.roll(base, -1, axis=0)
    tangent_gap = state_next[:, 0] - jnp.roll(state[:, 0], -1, axis=0)
    adjoint_gap = state_next[:, 1] - jnp.roll(state[:, 1], 1, axis=0)
    state_gap = jnp.stack([tangent_gap, adjoint_gap], axis=1)
    return base_gap.reshape(SEG, 3, N, N * N).astype(jnp.float32), state_gap.reshape(SEG, 2, 3, N, N * N).astype(jnp.float32)
```

```python
import functools

import jax
import jax.numpy as jnp
import ml_dtypes
import numpy as np
from jax import lax
from jax.experimental import pallas as pl
from jax.experimental.pallas import tpu as pltpu
from jax.sharding import PartitionSpec as P

N = 64
THIRD = N // 3
LOW = THIRD - 3
KZ = THIRD + 1
KP = 24
MP = 48
PAIRS = N // 2
viscosity = 0.025
time_step = 0.02
forcing_amp = 10.0
f32 = jnp.float32
bf16 = jnp.bfloat16

NN = (((1,), (0,)), ((), ()))
NT = (((1,), (1,)), ((), ()))
TN = (((0,), (0,)), ((), ()))


def split(value):
    high = value.astype(bf16)
    return high, (value - high.astype(f32)).astype(bf16)


def dot3(left, right, dims):
    dot = functools.partial(lax.dot_general, dimension_numbers=dims, preferred_element_type=f32)
    return dot(left[0], right[0]) + (dot(left[0], right[1]) + dot(left[1], right[0]))


def table(values):
    values = np.asarray(values, np.float32)
    high = values.astype(ml_dtypes.bfloat16)
    low = (values - high.astype(np.float32)).astype(ml_dtypes.bfloat16)
    return np.stack([high, low], axis=-3)


def signed():
    m = np.arange(2 * THIRD + 1)
    return np.where(m <= THIRD, m, m - (2 * THIRD + 1))


def angles(first, second):
    return np.mod(np.outer(first, second), N) * (2 * np.pi / N)


def cuts():
    return range(LOW, THIRD + 1)


def z_tables():
    plain, ik = [], []
    k = np.arange(KZ)
    a = angles(k, np.arange(N))
    for cut in cuts():
        keep = 1.0 * (k <= cut)[:, None]
        w = np.zeros((2, KP, N))
        v = np.zeros((2, KP, N))
        w[0, :KZ], w[1, :KZ] = keep * np.cos(a), -keep * np.sin(a)
        v[0, :KZ], v[1, :KZ] = keep * k[:, None] * np.sin(a), keep * k[:, None] * np.cos(a)
        plain.append(np.kron(np.eye(2), w.reshape(2 * KP, N)))
        ik.append(np.kron(np.eye(2), v.reshape(2 * KP, N)))
    return table(np.stack([np.stack(plain), np.stack(ik)], axis=1))


def y_tables():
    out = []
    m = signed()
    count = len(m)
    a = angles(m, np.arange(N))
    for cut in cuts():
        keep = 1.0 * (np.abs(m) <= cut)[:, None]
        c, s = keep * np.cos(a), keep * np.sin(a)
        w = np.zeros((2, MP, N, 2))
        w[0, :count, :, 0], w[0, :count, :, 1] = c, s
        w[1, :count, :, 0], w[1, :count, :, 1] = -s, c
        v = np.zeros_like(w)
        v[0, :count] = -m[:, None, None] * w[1, :count]
        v[1, :count] = m[:, None, None] * w[0, :count]
        out.append(np.stack([w.reshape(2 * MP, 2 * N), v.reshape(2 * MP, 2 * N)]))
    return table(np.stack(out))


def y_back():
    m = signed()
    count = len(m)
    a = angles(np.arange(N), m)
    c, s = np.cos(a) / N, np.sin(a) / N
    w = np.zeros((N, 2, 2, MP))
    w[:, 0, 0, :count], w[:, 0, 1, :count] = c, -s
    w[:, 1, 0, :count], w[:, 1, 1, :count] = s, c
    v = np.zeros_like(w)
    v[:, :, 0, :count] = m * w[:, :, 1, :count]
    v[:, :, 1, :count] = -m * w[:, :, 0, :count]
    return table(np.stack([w.reshape(2 * N, 2 * MP), v.reshape(2 * N, 2 * MP)]))


def z_back():
    k = np.arange(KZ)
    a = angles(k, np.arange(N))
    weight = (np.where(k == 0, 1.0, 2.0) / N)[:, None]
    w = np.zeros((2, KP, N))
    w[0, :KZ], w[1, :KZ] = weight * np.cos(a), -weight * np.sin(a)
    v = np.zeros_like(w)
    v[0, :KZ] = k[:, None] * w[1, :KZ]
    v[1, :KZ] = -k[:, None] * w[0, :KZ]
    pair = lambda t: np.kron(np.eye(2), t.reshape(2 * KP, N))
    return table(np.stack([pair(w), pair(v)]))


def x_filters(slabs):
    rows = N // slabs
    out = []
    x = np.arange(N)
    for cut in cuts():
        n = np.arange(-cut, cut + 1)
        d = np.mod(x[:, None] - x[None, :], N)
        phase = 2 * np.pi / N * n[:, None, None] * -d
        plain = np.cos(phase).sum(0) / N
        deriv = (-n[:, None, None] * np.sin(phase)).sum(0) / N
        both = np.stack([plain, deriv]).reshape(2, slabs, rows, slabs, rows)
        wide = np.zeros((slabs, 2, slabs, 3, rows, 3, rows))
        for i in range(3):
            wide[:, :, :, i, :, i, :] = both.transpose(3, 0, 1, 2, 4)
        out.append(wide.reshape(slabs, 2, slabs, 3 * rows, 3 * rows))
    return table(np.stack(out))


def x_tables(slabs):
    rows = N // slabs
    n = signed()
    count = len(n)
    a = angles(np.arange(N), n).reshape(slabs, rows, count)
    out = []
    for cut in cuts():
        keep = 1.0 * (np.abs(n) <= cut)
        c, s = np.cos(a) * keep, np.sin(a) * keep
        w = np.zeros((slabs, 2, 2, 3, rows, 3, 2, 64))
        for i in range(3):
            w[:, 0, 0, i, :, i, 0, :count] = c
            w[:, 0, 0, i, :, i, 1, :count] = -s
            w[:, 0, 1, i, :, i, 0, :count] = s
            w[:, 0, 1, i, :, i, 1, :count] = c
        w[:, 1, :, :, :, :, 0, :count] = -n * w[:, 0, :, :, :, :, 1, :count]
        w[:, 1, :, :, :, :, 1, :count] = n * w[:, 0, :, :, :, :, 0, :count]
        out.append(w.reshape(slabs, 2, 2, 3 * rows, 384))
    return table(np.stack(out))


def x_back(slabs):
    rows = N // slabs
    n = signed()
    count = len(n)
    a = angles(n, np.arange(N)).reshape(count, slabs, rows).transpose(1, 0, 2)
    c, s = np.cos(a) / N, np.sin(a) / N
    w = np.zeros((slabs, 2, 3, 2, 64, 3, rows))
    for i in range(3):
        w[:, 0, i, 0, :count, i] = c
        w[:, 0, i, 1, :count, i] = -s
        w[:, 1, i, 0, :count, i] = s
        w[:, 1, i, 1, :count, i] = c
    return table(w.reshape(slabs, 2, 384, 3 * rows))


def both(ref, *index):
    return ref[(*index, 0)], ref[(*index, 1)]


def lanes(p):
    return pl.ds(pl.multiple_of(p * 128, 128), 128)


def pair_rows(p):
    return pl.ds(pl.multiple_of(p * 4 * KP, 8), 4 * KP)


def column(k):
    return pl.ds(k, 2 * N, stride=KP)


def flat(block):
    return block.reshape(block.shape[0] * block.shape[1], block.shape[2])


def loop(count, unroll, step):
    def go(i, carry):
        step(i)
        return carry

    lax.fori_loop(0, count, go, 0, unroll=unroll)


def base_ahead(base_ref, wz_ref, wy_ref, out_ref, work):
    def along_z(p):
        block = split(flat(base_ref[:, :, lanes(p)]))
        work[pair_rows(p), :] = dot3(both(wz_ref, 0), block, NT)

    loop(PAIRS, 4, along_z)

    def along_y(k):
        out_ref[k] = dot3(both(wy_ref, 0), split(work[column(k), :]), NN)

    loop(KZ, 2, along_y)


def flux_ahead(base_ref, state_ref, wz_ref, wy_ref, g_ref, f_ref, work_a, work_b, work_f):
    scale = jnp.where(lax.axis_index("comp") == 0, -time_step, time_step).astype(f32)

    def along_z(p):
        state = state_ref[:, :, lanes(p)]
        base = base_ref[:, :, lanes(p)]
        scaled = state * scale
        f0, f1, f2 = (split(flat(scaled * base[j][None])) for j in range(3))
        plain = both(wz_ref, 0)
        work_a[pair_rows(p), :] = dot3(plain, split(flat(state)), NT) + dot3(
            both(wz_ref, 1), f2, NT
        )
        work_b[pair_rows(p), :] = dot3(plain, f1, NT)
        work_f[pair_rows(p), :] = dot3(plain, f0, NT)

    loop(PAIRS, 2, along_z)

    def along_y(k):
        plain = both(wy_ref, 0)
        g_ref[k] = dot3(plain, split(work_a[column(k), :]), NN) + dot3(
            both(wy_ref, 1), split(work_b[column(k), :]), NN
        )
        f_ref[k] = dot3(plain, split(work_f[column(k), :]), NN)

    loop(KZ, 2, along_y)


def gradients(
    slabs, got_ref, base_ref, state_ref, force_ref, pd_ref, yb_ref, zb_ref, wz_ref, wy_ref,
    xt_ref, g_ref, f_ref, out_ref, base_out_ref, work_0, work_1, work_2,
):
    tangent = lax.axis_index("comp") == 0

    def back_y(k):
        sources = [split(got_ref[s, k]) for s in range(slabs)]

        def across(kind):
            total = dot3(sources[0], both(pd_ref, kind, 0), NN)
            for s in range(1, slabs):
                total = total + dot3(sources[s], both(pd_ref, kind, s), NN)
            return split(total)

        plain, deriv = across(0), across(1)
        work_0[column(k), :] = dot3(both(yb_ref, 0), deriv, NN)
        work_1[column(k), :] = dot3(both(yb_ref, 1), plain, NN)
        work_2[column(k), :] = dot3(both(yb_ref, 0), plain, NN)

    def clear(p):
        zero = jnp.zeros((4 * KP, work_0.shape[1]), f32)
        work_0[pair_rows(p), :] = zero
        work_1[pair_rows(p), :] = zero
        work_2[pair_rows(p), :] = zero

    loop(PAIRS, 2, clear)
    loop(KZ, 2, back_y)

    def grid_space(p):
        state = state_ref[:, :, lanes(p)]
        base = base_ref[:, :, lanes(p)]
        grad = []
        for work, kind in ((work_0, 0), (work_1, 0), (work_2, 1)):
            rows = dot3(split(work[pair_rows(p), :]), both(zb_ref, kind), TN)
            grad.append(rows.reshape(base.shape))
        coupled, driven = [], []
        for i in range(3):
            total = 0.0
            drive = 0.0
            for j in range(3):
                total = total + jnp.where(tangent, grad[j][i], grad[i][j]) * state[j]
                drive = drive + grad[j][i] * base[j]
            if i == 0:
                drive = drive - force_ref[:, lanes(p)]
            coupled.append(-time_step * total)
            driven.append(base[i] - time_step * drive)
        plain = both(wz_ref, 0)
        work_0[pair_rows(p), :] = dot3(plain, split(jnp.concatenate(coupled, axis=0)), NT)
        work_1[pair_rows(p), :] = dot3(plain, split(jnp.concatenate(driven, axis=0)), NT)

    loop(PAIRS, 2, grid_space)

    def ahead_x(k):
        plain = both(wy_ref, 0)
        total = g_ref[k] + dot3(plain, split(work_0[column(k), :]), NN)
        driven = dot3(plain, split(work_1[column(k), :]), NN)
        outer = f_ref[k]
        state_modes, base_modes = 0.0, 0.0
        for d in range(2):
            rows = slice(d * MP, (d + 1) * MP)
            state_modes = state_modes + dot3(split(total[rows]), both(xt_ref, 0, d), NN)
            state_modes = state_modes + dot3(split(outer[rows]), both(xt_ref, 1, d), NN)
            base_modes = base_modes + dot3(split(driven[rows]), both(xt_ref, 0, d), NN)
        out_ref[k] = state_modes
        base_out_ref[k] = base_modes

    loop(KZ, 2, ahead_x)


def finish(count, *refs):
    parts, (near_ref, xb_ref, yb_ref, zb_ref, out_ref, work) = refs[:count], refs[count:]
    column_n = lax.rem(lax.broadcasted_iota(jnp.int32, (MP, 128), 1), 64)
    row_m = lax.broadcasted_iota(jnp.int32, (MP, 128), 0)
    wrap = lambda v: jnp.where(v <= THIRD, v, v - (2 * THIRD + 1)).astype(f32)
    wave_x, wave_y = wrap(column_n), wrap(row_m)
    flat_square = wave_x * wave_x + wave_y * wave_y

    def clear(p):
        work[pair_rows(p), :] = jnp.zeros((4 * KP, work.shape[1]), f32)

    loop(PAIRS, 2, clear)

    def spectral(k):
        modes = parts[0][k]
        for part in parts[1:]:
            modes = modes + part[k]
        wave_z = jnp.asarray(k, jnp.int32).astype(f32)
        square = flat_square + wave_z * wave_z
        safe = jnp.where(square > 0, square, 1.0)
        damping = 1.0 / (1.0 + viscosity * time_step * square)
        w = [modes[:, i * 128 : (i + 1) * 128] for i in range(3)]
        divergence = (wave_x * w[0] + wave_y * w[1] + wave_z * w[2]) / safe
        new = [
            damping * (w[0] - wave_x * divergence),
            damping * (w[1] - wave_y * divergence),
            damping * (w[2] - wave_z * divergence),
        ]
        new = split(jnp.concatenate(new, axis=1))
        rows = [dot3(new, both(xb_ref, d), NN) for d in range(2)]
        work[column(k), :] = dot3(both(yb_ref, 0), split(jnp.concatenate(rows, axis=0)), NN)

    loop(KZ, 2, spectral)

    def along_z(p):
        rows = dot3(split(work[pair_rows(p), :]), both(zb_ref, 0), TN)
        near = near_ref[:, :, lanes(p)]
        out_ref[:, :, lanes(p)] = rows.reshape(near.shape) - near

    loop(PAIRS, 4, along_z)


def call(kernel, out_shape, scratch, cost, *operands):
    return pl.pallas_call(
        kernel,
        out_shape=out_shape,
        in_specs=[pl.BlockSpec(memory_space=pltpu.VMEM)] * len(operands),
        out_specs=jax.tree.map(lambda _: pl.BlockSpec(memory_space=pltpu.VMEM), out_shape),
        scratch_shapes=scratch,
        compiler_params=pltpu.CompilerParams(vmem_limit_bytes=48 * 2**20),
        cost_estimate=pl.CostEstimate(flops=cost, bytes_accessed=8 * 2**20, transcendentals=0),
    )(*operands)


def body(base, state, wavenumber, cutoff):
    base, state = base[0], state[0, 0]
    slab_rows = base.shape[1]
    half = slab_rows // lax.axis_size("comp")
    slabs = lax.axis_size("slab")
    segs = lax.axis_size("seg")
    slab = lax.axis_index("slab")
    side = lax.axis_index("comp")
    width = 3 * slab_rows
    which = cutoff - LOW

    route = [((s, 0), ((s - 1) % segs, 0)) for s in range(segs)]
    route += [((s, 1), ((s + 1) % segs, 1)) for s in range(segs)]
    route = [(a * 2 + b, c * 2 + d) for (a, b), (c, d) in route]
    near_state = lax.ppermute(state, ("seg", "comp"), route)
    base_half = lax.dynamic_slice_in_dim(base, side * half, half, 1)
    near_base = lax.ppermute(base_half, "seg", [((s + 1) % segs, s) for s in range(segs)])

    wz = lax.dynamic_index_in_dim(jnp.asarray(z_tables()), which[2], 0, False)
    wy = lax.dynamic_index_in_dim(jnp.asarray(y_tables()), which[1], 0, False)
    filters, ahead = jnp.asarray(x_filters(slabs)), jnp.asarray(x_tables(slabs))
    pick = lambda t: lax.dynamic_slice(
        t, (which[0], slab) + (0,) * (t.ndim - 2), (1, 1) + t.shape[2:]
    )[0, 0]
    pd, xt = pick(filters), pick(ahead)
    xb = lax.dynamic_index_in_dim(jnp.asarray(x_back(slabs)), slab, 0, False)
    yb, zb = jnp.asarray(y_back()), jnp.asarray(z_back())

    modes = jax.ShapeDtypeStruct((KZ, 2 * MP, width), f32)
    spectrum = jax.ShapeDtypeStruct((KZ, MP, 384), f32)
    work = pltpu.VMEM((2 * N * KP, width), f32)
    own = call(base_ahead, modes, [work], 10**9, base, wz, wy)
    if slabs == 2:
        other = lax.ppermute(own, "slab", [(0, 1), (1, 0)])
        first = slab == 0
        got = jnp.stack([own, other])
        pd = jnp.where(first, pd, pd[:, ::-1])
    else:
        got = lax.all_gather(own, "slab")
    g, f = call(flux_ahead, (modes, modes), [work] * 3, 4 * 10**9, base, state, wz, wy)

    y = jnp.arange(N, dtype=jnp.int32)
    phase = jnp.mod(wavenumber[0] * y, N).astype(f32) * (2.0 * jnp.pi / N)
    force = jnp.repeat(forcing_amp * jnp.sin(phase), N)[None]
    state_modes, base_modes = call(
        functools.partial(gradients, slabs), (spectrum, spectrum), [work] * 3, 8 * 10**9,
        got, base, state, force, pd, yb, zb, wz, wy, xt, g, f,
    )
    if slabs == 2:
        swap = lambda v: lax.ppermute(v, "slab", [(0, 1), (1, 0)])
        state_parts = (state_modes, swap(state_modes))
        base_parts = (base_modes, swap(base_modes))
    else:
        state_parts = (lax.psum(state_modes, "slab"),)
        base_parts = (lax.psum(base_modes, "slab"),)

    shape = jax.ShapeDtypeStruct(base.shape, f32)
    last = functools.partial(finish, len(state_parts))
    near_wide = jnp.concatenate([near_base, near_base], axis=1)
    base_gap = call(last, shape, [work], 10**9, *base_parts, near_wide, xb, yb, zb)
    base_gap = lax.dynamic_slice_in_dim(base_gap, side * half, half, 1)
    state_gap = call(last, shape, [work], 10**9, *state_parts, near_state, xb, yb, zb)
    return base_gap[None], state_gap[None, None]


def solution(mesh):
    return jax.shard_map(
        body,
        mesh=mesh,
        in_specs=(
            P(("groups", "seg"), None, "slab", None),
            P(("groups", "seg"), "comp", None, "slab", None),
            P("groups"),
            P("groups"),
        ),
        out_specs=(
            P(("groups", "seg"), None, ("slab", "comp"), None),
            P(("groups", "seg"), "comp", None, "slab", None),
        ),
        check_vma=False,
    )
```

```python
import functools

import jax
import jax.numpy as jnp
import ml_dtypes
import numpy as np
from jax import lax
from jax.experimental import pallas as pl
from jax.experimental.pallas import tpu as pltpu
from jax.sharding import PartitionSpec as P

N = 64
BACK, GRID, AHEAD, SPEC, Z1, Z2, Z3, Y1 = 4, 4, 4, 4, 8, 4, 8, 6
THIRD = N // 3
LOW = THIRD - 3
KZ = THIRD + 1
KP = 24
MP = 48
PAIRS = N // 2
FLUX = 14 * 10**9
HALF = KZ // 2
viscosity = 0.025
time_step = 0.02
forcing_amp = 10.0
f32 = jnp.float32
bf16 = jnp.bfloat16

NN = (((1,), (0,)), ((), ()))
NT = (((1,), (1,)), ((), ()))


def split(value):
    high = value.astype(bf16)
    return high, (value - high.astype(f32)).astype(bf16)


def dot3(left, right, dims):
    dot = functools.partial(lax.dot_general, dimension_numbers=dims, preferred_element_type=f32)
    return dot(left[0], right[0]) + (dot(left[0], right[1]) + dot(left[1], right[0]))


def table(values):
    values = np.asarray(values, np.float32)
    high = values.astype(ml_dtypes.bfloat16)
    low = (values - high.astype(np.float32)).astype(ml_dtypes.bfloat16)
    return np.stack([high, low], axis=-3)


def table3(values):
    high, low = np.moveaxis(table(values), -3, 0)
    return np.concatenate([high, high, low], axis=-1)


def left3(left, value, dims):
    high, low = split(value)
    deep = jnp.concatenate([high, low, high], axis=dims[0][1][0])
    return lax.dot_general(left, deep, dimension_numbers=dims, preferred_element_type=f32)


def signed():
    m = np.arange(2 * THIRD + 1)
    return np.where(m <= THIRD, m, m - (2 * THIRD + 1))


def angles(first, second):
    return np.mod(np.outer(first, second), N) * (2 * np.pi / N)


def cuts():
    return range(LOW, THIRD + 1)


def z_tables():
    plain, ik = [], []
    k = np.arange(KZ)
    a = angles(k, np.arange(N))
    for cut in cuts():
        keep = 1.0 * (k <= cut)[:, None]
        w = np.zeros((2, KP, N))
        v = np.zeros((2, KP, N))
        w[0, :KZ], w[1, :KZ] = keep * np.cos(a), -keep * np.sin(a)
        v[0, :KZ], v[1, :KZ] = keep * k[:, None] * np.sin(a), keep * k[:, None] * np.cos(a)
        plain.append(np.kron(np.eye(2), w.reshape(2 * KP, N)))
        ik.append(np.kron(np.eye(2), v.reshape(2 * KP, N)))
    return table3(np.stack([np.stack(plain), np.stack(ik)], axis=1))


def y_tables():
    out = []
    m = signed()
    count = len(m)
    a = angles(m, np.arange(N))
    for cut in cuts():
        keep = 1.0 * (np.abs(m) <= cut)[:, None]
        c, s = keep * np.cos(a), keep * np.sin(a)
        w = np.zeros((2, MP, N, 2))
        w[0, :count, :, 0], w[0, :count, :, 1] = c, s
        w[1, :count, :, 0], w[1, :count, :, 1] = -s, c
        v = np.zeros_like(w)
        v[0, :count] = -m[:, None, None] * w[1, :count]
        v[1, :count] = m[:, None, None] * w[0, :count]
        out.append(np.stack([w.reshape(2 * MP, 2 * N), v.reshape(2 * MP, 2 * N)]))
    return table3(np.stack(out))


def y_back():
    m = signed()
    count = len(m)
    a = angles(np.arange(N), m)
    c, s = np.cos(a) / N, np.sin(a) / N
    w = np.zeros((N, 2, 2, MP))
    w[:, 0, 0, :count], w[:, 0, 1, :count] = c, -s
    w[:, 1, 0, :count], w[:, 1, 1, :count] = s, c
    v = np.zeros_like(w)
    v[:, :, 0, :count] = m * w[:, :, 1, :count]
    v[:, :, 1, :count] = -m * w[:, :, 0, :count]
    return table3(np.stack([w.reshape(2 * N, 2 * MP), v.reshape(2 * N, 2 * MP)]))


def z_back():
    k = np.arange(KZ)
    a = angles(k, np.arange(N))
    weight = (np.where(k == 0, 1.0, 2.0) / N)[:, None]
    w = np.zeros((2, KP, N))
    w[0, :KZ], w[1, :KZ] = weight * np.cos(a), -weight * np.sin(a)
    v = np.zeros_like(w)
    v[0, :KZ] = k[:, None] * w[1, :KZ]
    v[1, :KZ] = -k[:, None] * w[0, :KZ]
    pair = lambda t: np.kron(np.eye(2), t.reshape(2 * KP, N))
    return table3(np.stack([pair(w).T, pair(v).T]))


def x_filters(slabs):
    rows = N // slabs
    out = []
    x = np.arange(N)
    for cut in cuts():
        n = np.arange(-cut, cut + 1)
        d = np.mod(x[:, None] - x[None, :], N)
        phase = 2 * np.pi / N * n[:, None, None] * -d
        plain = np.cos(phase).sum(0) / N
        deriv = (-n[:, None, None] * np.sin(phase)).sum(0) / N
        both = np.stack([plain, deriv]).reshape(2, slabs, rows, slabs, rows)
        wide = np.zeros((slabs, 2, slabs, 3, rows, 3, rows))
        for i in range(3):
            wide[:, :, :, i, :, i, :] = both.transpose(3, 0, 1, 2, 4)
        out.append(wide.reshape(slabs, 2, slabs, 3 * rows, 3 * rows))
    return table(np.stack(out))


def x_tables(slabs):
    rows = N // slabs
    n = signed()
    count = len(n)
    a = angles(np.arange(N), n).reshape(slabs, rows, count)
    out = []
    for cut in cuts():
        keep = 1.0 * (np.abs(n) <= cut)
        c, s = np.cos(a) * keep, np.sin(a) * keep
        w = np.zeros((slabs, 2, 2, 3, rows, 3, 2, 64))
        for i in range(3):
            w[:, 0, 0, i, :, i, 0, :count] = c
            w[:, 0, 0, i, :, i, 1, :count] = -s
            w[:, 0, 1, i, :, i, 0, :count] = s
            w[:, 0, 1, i, :, i, 1, :count] = c
        w[:, 1, :, :, :, :, 0, :count] = -n * w[:, 0, :, :, :, :, 1, :count]
        w[:, 1, :, :, :, :, 1, :count] = n * w[:, 0, :, :, :, :, 0, :count]
        out.append(w.reshape(slabs, 2, 2, 3 * rows, 384))
    return table(np.stack(out))


def x_back(slabs):
    rows = N // slabs
    n = signed()
    count = len(n)
    a = angles(n, np.arange(N)).reshape(count, slabs, rows).transpose(1, 0, 2)
    c, s = np.cos(a) / N, np.sin(a) / N
    w = np.zeros((slabs, 2, 3, 2, 64, 3, rows))
    for i in range(3):
        w[:, 0, i, 0, :count, i] = c
        w[:, 0, i, 1, :count, i] = -s
        w[:, 1, i, 0, :count, i] = s
        w[:, 1, i, 1, :count, i] = c
    return table(w.reshape(slabs, 2, 384, 3 * rows))


def both(ref, *index):
    return ref[(*index, 0)], ref[(*index, 1)]


def lanes(p):
    return pl.ds(pl.multiple_of(p * 128, 128), 128)


def pair_rows(p):
    return pl.ds(pl.multiple_of(p * 4 * KP, 8), 4 * KP)


def column(k):
    return pl.ds(k, 2 * N, stride=KP)


def flat(block):
    return block.reshape(block.shape[0] * block.shape[1], block.shape[2])


def loop(count, unroll, step):
    def go(i, carry):
        step(i)
        return carry

    lax.fori_loop(0, count, go, 0, unroll=unroll)


def clear_padding(*works):
    for k in range(KZ, KP):
        for work in works:
            work[column(k), :] = jnp.zeros((2 * N, work.shape[1]), f32)


def base_ahead(base_ref, wz_ref, wy_ref, out_ref, half_ref, work):
    def along_z(p):
        work[pair_rows(p), :] = left3(wz_ref[0], flat(base_ref[:, :, lanes(p)]), NT)

    loop(PAIRS, Z1, along_z)

    def along_y(k):
        out_ref[k] = left3(wy_ref[0], work[column(k), :], NN)

    loop(KZ, Y1, along_y)
    first = HALF * lax.axis_index("comp")

    def share(j):
        half_ref[j] = out_ref[first + j]

    loop(HALF, 1, share)


def sign_step():
    return jnp.where(lax.axis_index("comp") == 0, -time_step, time_step).astype(f32)


def flux_ahead(base_ref, state_ref, wz_ref, wy_ref, g_ref, work_a, work_b):
    scale = sign_step()

    def along_z(p):
        state = state_ref[:, :, lanes(p)]
        scaled = state * scale
        f1, f2 = (flat(scaled * base_ref[j, :, lanes(p)][None]) for j in (1, 2))
        plain = wz_ref[0]
        work_a[pair_rows(p), :] = left3(plain, flat(state), NT) + left3(wz_ref[1], f2, NT)
        work_b[pair_rows(p), :] = left3(plain, f1, NT)

    loop(PAIRS, Z2, along_z)

    def along_y(k):
        g_ref[k] = left3(wy_ref[0], work_a[column(k), :], NN) + left3(
            wy_ref[1], work_b[column(k), :], NN
        )

    loop(KZ, Y1, along_y)


def flux_x_ahead(base_ref, state_ref, wz_ref, wy_ref, f_ref, work):
    scale = sign_step()

    def along_z(p):
        f0 = flat(state_ref[:, :, lanes(p)] * scale * base_ref[0, :, lanes(p)][None])
        work[pair_rows(p), :] = left3(wz_ref[0], f0, NT)

    loop(PAIRS, Z2, along_z)

    def along_y(k):
        f_ref[k] = left3(wy_ref[0], work[column(k), :], NN)

    loop(KZ, Y1, along_y)


def gradients(
    slabs, count, *refs,
):
    got, rest = refs[:count], refs[count:]
    side = lax.axis_index("comp")
    if count == 1:
        visits = [(lambda j: (j, [got[0][s, j] for s in range(slabs)]), KZ)]
    else:
        own, mine, partner = got

        def visit(ref, first):
            return lambda j: (first + j, [own[first + j], ref[j]])

        visits = [
            (visit(mine, HALF * side), HALF),
            (visit(partner, HALF * (1 - side)), HALF),
        ]
    gradients_of(slabs, visits, *rest)


def gradients_of(
    slabs, visits, base_ref, state_ref, force_ref, pd_ref, yb_ref, zb_ref, wz_ref, wy_ref,
    xt_ref, base_out_ref, coupled_ref, work_0, work_1, work_2,
):
    tangent = lax.axis_index("comp") == 0

    def back_y(visit, j):
        k, sources = visit(j)
        sources = [split(source) for source in sources]

        def across(kind):
            total = dot3(sources[0], both(pd_ref, kind, 0), NN)
            for s in range(1, slabs):
                total = total + dot3(sources[s], both(pd_ref, kind, s), NN)
            return total

        plain, deriv = across(0), across(1)
        work_0[column(k), :] = left3(yb_ref[0], deriv, NN)
        work_1[column(k), :] = left3(yb_ref[1], plain, NN)
        work_2[column(k), :] = left3(yb_ref[0], plain, NN)

    clear_padding(work_0, work_1, work_2)
    for visit, count in visits:
        loop(count, BACK, functools.partial(back_y, visit))

    def grid_space(p):
        state = state_ref[:, :, lanes(p)]
        base = base_ref[:, :, lanes(p)]
        grad = []
        for work, kind in ((work_0, 0), (work_1, 0), (work_2, 1)):
            rows = left3(zb_ref[kind], work[pair_rows(p), :], NN).T
            grad.append(rows.reshape(base.shape))
        coupled, driven = [], []
        for i in range(3):
            total = 0.0
            drive = 0.0
            for j in range(3):
                total = total + jnp.where(tangent, grad[j][i], grad[i][j]) * state[j]
                drive = drive + grad[j][i] * base[j]
            if i == 0:
                drive = drive - force_ref[:, lanes(p)]
            coupled.append(-time_step * total)
            driven.append(base[i] - time_step * drive)
        plain = wz_ref[0]
        coupled_ref[pair_rows(p), :] = left3(plain, jnp.concatenate(coupled, axis=0), NT)
        work_1[pair_rows(p), :] = left3(plain, jnp.concatenate(driven, axis=0), NT)

    loop(PAIRS, GRID, grid_space)

    waves = plane_waves()
    first = HALF * lax.axis_index("comp")

    def base_ahead_x(step):
        j = HALF - 1 - step
        k = first + j
        driven = left3(wy_ref[0], work_1[column(k), :], NN)
        modes = 0.0
        for d in range(2):
            rows = slice(d * MP, (d + 1) * MP)
            modes = modes + dot3(split(driven[rows]), both(xt_ref, 0, d), NN)
        emit(waves, base_out_ref, j, HALF, modes, k)

    loop(HALF, AHEAD, base_ahead_x)


def emit(waves, ref, slot, last, modes, k):
    new = projected(waves, modes, k)
    ref[slot] = jnp.concatenate(new[:2], axis=1)
    ref[last] = jnp.concatenate([new[2], jnp.zeros_like(new[2])], axis=1)


def state_ahead_x(coupled_ref, wy_ref, xt_ref, g_ref, f_ref, out_ref):
    waves = plane_waves()

    def ahead_x(step):
        k = KZ - 1 - step
        total = g_ref[k] + left3(wy_ref[0], coupled_ref[column(k), :], NN)
        outer = f_ref[k]
        modes = 0.0
        for d in range(2):
            rows = slice(d * MP, (d + 1) * MP)
            modes = modes + dot3(split(total[rows]), both(xt_ref, 0, d), NN)
            modes = modes + dot3(split(outer[rows]), both(xt_ref, 1, d), NN)
        emit(waves, out_ref, k, KZ, modes, k)

    loop(KZ, AHEAD, ahead_x)


def plane_waves():
    column_n = lax.rem(lax.broadcasted_iota(jnp.int32, (MP, 128), 1), 64)
    row_m = lax.broadcasted_iota(jnp.int32, (MP, 128), 0)
    wrap = lambda v: jnp.where(v <= THIRD, v, v - (2 * THIRD + 1)).astype(f32)
    return wrap(column_n), wrap(row_m)


def projected(waves, modes, k):
    wave_x, wave_y = waves
    wave_z = jnp.asarray(k, jnp.int32).astype(f32)
    square = wave_x * wave_x + wave_y * wave_y + wave_z * wave_z
    safe = jnp.where(square > 0, square, 1.0)
    damping = 1.0 / (1.0 + viscosity * time_step * square)
    w = [modes[:, i * 128 : (i + 1) * 128] for i in range(3)]
    divergence = (wave_x * w[0] + wave_y * w[1] + wave_z * w[2]) / safe
    return [
        damping * (w[0] - wave_x * divergence),
        damping * (w[1] - wave_y * divergence),
        damping * (w[2] - wave_z * divergence),
    ]


def finish(count, halved, *refs):
    parts, (near_ref, xb_ref, yb_ref, zb_ref, out_ref, work) = refs[:count], refs[count:]
    wave_x, wave_y = plane_waves()
    clear_padding(work)

    def spectral(parts, first, last, j):
        k = first + j
        modes, third = 0.0, 0.0
        for part in parts:
            modes = modes + part[j]
            third = third + part[last, :, :128]
        w0, w1 = modes[:, :128], modes[:, 128:]
        whole = jnp.asarray(k, jnp.int32)
        inverse = 1.0 / jnp.maximum(whole, 1).astype(f32)
        w2 = jnp.where(whole == 0, third, -(wave_x * w0 + wave_y * w1) * inverse)
        new = split(jnp.concatenate([w0, w1, w2], axis=1))
        rows = [dot3(new, both(xb_ref, d), NN) for d in range(2)]
        work[column(k), :] = left3(yb_ref[0], jnp.concatenate(rows, axis=0), NN)

    if halved:
        side = lax.axis_index("comp")
        for part, place in zip(parts, (side, 1 - side)):
            loop(HALF, SPEC, functools.partial(spectral, [part], HALF * place, HALF))
    else:
        loop(KZ, SPEC, functools.partial(spectral, parts, 0, KZ))

    def along_z(p):
        rows = left3(zb_ref[0], work[pair_rows(p), :], NN).T
        near = near_ref[:, :, lanes(p)]
        out_ref[:, :, lanes(p)] = rows.reshape(near.shape) - near

    loop(PAIRS, Z3, along_z)


def call(kernel, out_shape, scratch, cost, *operands):
    return pl.pallas_call(
        kernel,
        out_shape=out_shape,
        in_specs=[pl.BlockSpec(memory_space=pltpu.VMEM)] * len(operands),
        out_specs=jax.tree.map(lambda _: pl.BlockSpec(memory_space=pltpu.VMEM), out_shape),
        scratch_shapes=scratch,
        compiler_params=pltpu.CompilerParams(vmem_limit_bytes=48 * 2**20),
        cost_estimate=pl.CostEstimate(flops=cost, bytes_accessed=2**10, transcendentals=0),
    )(*operands)


def body(base, state, wavenumber, cutoff):
    base, state = base[0], state[0, 0]
    slab_rows = base.shape[1]
    half = slab_rows // lax.axis_size("comp")
    slabs = lax.axis_size("slab")
    segs = lax.axis_size("seg")
    slab = lax.axis_index("slab")
    side = lax.axis_index("comp")
    width = 3 * slab_rows
    which = cutoff - LOW

    route = [((s, 0), ((s - 1) % segs, 0)) for s in range(segs)]
    route += [((s, 1), ((s + 1) % segs, 1)) for s in range(segs)]
    route = [(a * 2 + b, c * 2 + d) for (a, b), (c, d) in route]
    wz = lax.dynamic_index_in_dim(jnp.asarray(z_tables()), which[2], 0, False)
    wy = lax.dynamic_index_in_dim(jnp.asarray(y_tables()), which[1], 0, False)
    filters, ahead = jnp.asarray(x_filters(slabs)), jnp.asarray(x_tables(slabs))
    pick = lambda t: lax.dynamic_slice(
        t, (which[0], slab) + (0,) * (t.ndim - 2), (1, 1) + t.shape[2:]
    )[0, 0]
    pd, xt = pick(filters), pick(ahead)
    xb = lax.dynamic_index_in_dim(jnp.asarray(x_back(slabs)), slab, 0, False)
    yb, zb = jnp.asarray(y_back()), jnp.asarray(z_back())

    modes = jax.ShapeDtypeStruct((KZ, 2 * MP, width), f32)
    half_modes = jax.ShapeDtypeStruct((HALF, 2 * MP, width), f32)
    spectrum = jax.ShapeDtypeStruct((KZ + 1, MP, 256), f32)
    half_spectrum = jax.ShapeDtypeStruct((HALF + 1, MP, 256), f32)
    work = pltpu.VMEM((2 * N * KP, width), f32)
    own, share = call(base_ahead, (modes, half_modes), [work], 4 * 10**9, base, wz, wy)
    later, later_base, share = lax.optimization_barrier((state, base, share))
    near_state = lax.ppermute(later, ("seg", "comp"), route)
    base_half = lax.dynamic_slice_in_dim(later_base, side * half, half, 1)
    near_base = lax.ppermute(base_half, "seg", [((s + 1) % segs, s) for s in range(segs)])
    if slabs == 2:
        other = lax.ppermute(share, "slab", [(0, 1), (1, 0)])
        partner = lax.ppermute(other, "comp", [(0, 1), (1, 0)])
        first = slab == 0
        got = (own, other, partner)
        pd = jnp.where(first, pd, pd[:, ::-1])
    else:
        got = (lax.all_gather(own, "slab"),)
    g = call(flux_ahead, modes, [work] * 2, FLUX, base, state, wz, wy)
    f = call(flux_x_ahead, modes, [work], 10**9, base, state, wz, wy)

    *got, g, f = lax.optimization_barrier((*got, g, f))

    y = jnp.arange(N, dtype=jnp.int32)
    phase = jnp.mod(wavenumber[0] * y, N).astype(f32) * (2.0 * jnp.pi / N)
    force = jnp.repeat(forcing_amp * jnp.sin(phase), N)[None]
    lined = jax.ShapeDtypeStruct((2 * N * KP, width), f32)
    base_modes, coupled = call(
        functools.partial(gradients, slabs, len(got)), (half_spectrum, lined), [work] * 3,
        25 * 10**9, *got, base, state, force, pd, yb, zb, wz, wy, xt,
    )
    state_modes = call(state_ahead_x, spectrum, [], 3 * 10**9, coupled, wy, xt, g, f)
    near_state, near_base, state_modes = lax.optimization_barrier(
        (near_state, near_base, state_modes)
    )
    if slabs == 2:
        swap = lambda v: lax.ppermute(v, "slab", [(0, 1), (1, 0)])
        state_other = swap(state_modes)
        base_other, state_modes = lax.optimization_barrier((swap(base_modes), state_modes))
        base_sum = base_modes + base_other
        state_parts = (state_modes, state_other)
    else:
        base_sum = lax.psum(base_modes, "slab")
        state_parts = (lax.psum(state_modes, "slab"),)
    base_parts = (base_sum, lax.ppermute(base_sum, "comp", [(0, 1), (1, 0)]))

    shape = jax.ShapeDtypeStruct(base.shape, f32)
    last = functools.partial(finish, len(state_parts), False)
    last_base = functools.partial(finish, 2, True)
    near_wide = jnp.concatenate([near_base, near_base], axis=1)
    base_gap = call(last_base, shape, [work], 10**8, *base_parts, near_wide, xb, yb, zb)
    base_gap = lax.dynamic_slice_in_dim(base_gap, side * half, half, 1)
    state_gap = call(last, shape, [work], 10**10, *state_parts, near_state, xb, yb, zb)
    return base_gap[None], state_gap[None, None]


def solution(mesh):
    return jax.shard_map(
        body,
        mesh=mesh,
        in_specs=(
            P(("groups", "seg"), None, "slab", None),
            P(("groups", "seg"), "comp", None, "slab", None),
            P("groups"),
            P("groups"),
        ),
        out_specs=(
            P(("groups", "seg"), None, ("slab", "comp"), None),
            P(("groups", "seg"), "comp", None, "slab", None),
        ),
        check_vma=False,
    )
```
